32 devices in a mesh: grp: 2 (over y), seq: 4 (over z), head: 2 (over x), tp: 2 (over core).
Axes of the slice: x: 2, y: 2, z: 4, core: 2. Of those that a mesh axis runs over, the one named last changes fastest.
Arguments:
- queries: bfloat16 [16384, 16, 128], P(('grp', 'seq'), ('head', 'tp')), parts along dimension 0, may hold values from -6 to 6
- key_rows: bfloat16 [16384, 16, 128], P(('grp', 'seq'), ('head', 'tp')), parts along dimension 0, may hold values from -6 to 6
- values: bfloat16 [16384, 16, 128], P(('grp', 'seq'), ('head', 'tp')), parts along dimension 0, may hold values from -6 to 6
- log_decay: float32 [16, 16384], P(('head', 'tp'), ('grp', 'seq')), parts along dimension 1, may hold values from -1 to 0
- write_rate: float32 [16, 16384], P(('head', 'tp'), ('grp', 'seq')), parts along dimension 1, may hold values from 0.002 to 0.05
- router_weight: bfloat16 [16, 128, 256], P(('head', 'tp')), may hold values from -100 to 100
- teacher_logits: bfloat16 [8, 4, 4, 128, 256], P(('grp', 'seq'), ('head', 'tp')), parts along dimension 0, may hold values from -400 to 400
- span_length: int32 [8, 4, 128], P(('grp', 'seq'), ('head', 'tp')), parts along dimension 0, may hold values from 1 to 16, 512 in all within a row
- span_owner: int32 [8, 4, 128, 1], P(('grp', 'seq'), ('head', 'tp')), parts along dimension 0, may hold values from 0 to 3; in each aligned block of 128 rows (0 to 127, 128 to 255, ..., all dimensions but the last counted through in order) at most 128 rows name the same one
Outputs:
- grad_router: float32 [32, 128, 256], P(('grp', 'head', 'tp')), parts along dimension 0
- grad_heads: float32 [16384, 16, 128], P(('grp', 'seq'), ('head', 'tp')), parts along dimension 0
- mean_kl: float32 [2], P('grp'), parts along dimension 0
The draws below stay inside these ranges and needn't reach their ends.
There are 2 independent parts, one for each index of `grp`. The reference program is written for one: setup_inputs(seed, part) draws one part's arguments, and reference() takes and returns one part's arrays. A program takes and returns all parts, laid end to end along the dimension named above; an argument that names none is the same for every part. Nothing has to cross between parts.
Inputs may be any that keep to these rules, and one draw needn't show every extreme that they name: `span_length`: the lengths of one region sum to 512. `span_owner`: among the tokens of one region no owner is named more than 128 times; some owner is named exactly 128 times in some regions.
All inputs are finite; a program needn't handle non-finite values.
Results may differ from the reference program's by a relative error of at most 0.008.
Values may be sent and summed in bfloat16 or wider, within the bound.
A program may use at most 128 MiB of HBM per device.

```python
import math
import jax
import jax.numpy as jnp
import numpy as np
from jax import lax

HEADS = 16
DK = 128
E = 256
ROWS = 2048
MAXLEN = 16
OCTET_TOTAL = 8192
COLUMNS = 4
REGION = 512
TOK_REG = 128
CAP = 128
NTOK = 2048
N_SEQ = 4


def draw_log_decay(key, part):
    address_embeddings = jax.random.split(jax.random.fold_in(key, 11), 7)
    blocks_seq = OCTET_TOTAL // ROWS
    odds = 2
    fast = jax.random.randint(address_embeddings[0], (HEADS, 1), 0, odds) == 0
    fast_rate = jnp.exp(jax.random.uniform(address_embeddings[1], (HEADS, 1), minval=math.log(1.0 / 20.0), maxval=math.log(1.0 / 8.0)))
    slow_rate = jnp.exp(jax.random.uniform(address_embeddings[2], (HEADS, 1), minval=math.log(0.05), maxval=math.log(0.2))) / OCTET_TOTAL
    device_factor = jnp.exp(jax.random.uniform(address_embeddings[3], (HEADS, blocks_seq, 1), minval=-0.7, maxval=0.7))
    device_factor = jnp.broadcast_to(device_factor, (HEADS, blocks_seq, ROWS)).reshape(HEADS, OCTET_TOTAL)
    token_factor = jax.random.uniform(address_embeddings[4], (HEADS, OCTET_TOTAL), minval=0.5, maxval=1.5)
    rate = jnp.where(fast, fast_rate, slow_rate) * device_factor * token_factor
    spike_offset = jax.random.randint(address_embeddings[5], (3, 1), 0, OCTET_TOTAL)
    agreement_tally = jnp.sum((lax.broadcasted_iota(jnp.int32, (3, OCTET_TOTAL), 1) == spike_offset).astype(jnp.float32), axis=0)
    loss = jax.random.uniform(address_embeddings[6], (HEADS, 1), minval=0.2, maxval=0.4)
    return (agreement_tally[None, :] * jnp.log(1.0 - loss) - rate).astype(jnp.float32)


def draw_router_weight(key, part):
    address_embeddings = jax.random.split(jax.random.fold_in(key, 23), 1)
    shape = (HEADS, DK, E)
    weights = jax.random.normal(address_embeddings[0], shape) / math.sqrt(HEADS * DK)
    weights = jnp.clip(weights, -6.0 / math.sqrt(HEADS * DK), 6.0 / math.sqrt(HEADS * DK))
    return weights.astype(jnp.bfloat16)


def draw_teacher_logits(key, part):
    address_embeddings = jax.random.split(jax.random.fold_in(key, 37), 1)
    shape = (OCTET_TOTAL // ROWS, COLUMNS, OCTET_TOTAL // ROWS, CAP, E)
    logits = jnp.clip(3.0 * jax.random.normal(address_embeddings[0], shape), -20.0, 20.0)
    return logits.astype(jnp.bfloat16)


def steps_of(key, shape, pieces, low, largest):
    def one(position, blocks):
        heights = jax.random.uniform(jax.random.fold_in(jax.random.fold_in(key, 6), position), (blocks,), jnp.float32, low / len(pieces), largest / len(pieces))
        return jnp.repeat(jnp.exp(heights), shape[position] // blocks).reshape((-1,) + (1,) * (len(shape) - position - 1))

    loudness = one(*pieces[0])
    for cut in pieces[1:]:
        loudness = loudness * one(*cut)
    return loudness


def split_up(amount, total, most, slope):
    loads = [(1 << 20) // math.isqrt(grade ** slope) + 1 for grade in range(2, amount + 1)]
    spare, given = total - most - (amount - 1), [1] * (amount - 1)
    while spare > 0:
        candidates = [i for i in range(amount - 1) if given[i] < most]
        whole, left = sum([loads[i] for i in candidates]), spare
        for i in candidates:
            addition = min(most - given[i], max(1, left * loads[i] // whole), spare)
            given[i] = given[i] + addition
            spare = spare - addition
    return np.array([most] + given)


def uneven(key, amount, total, bound, skew):
    if amount == 2:
        one = jax.random.randint(key, (), max(1, total - bound), min(bound, total - 1) + 1)
        return jnp.stack([one, total - one])
    sizes = jnp.asarray(split_up(amount, total, bound, skew), jnp.int32)
    pairs = (amount - 1) // 2
    source_of, receiver = sizes[1:1 + 2 * pairs:2], sizes[2:2 + 2 * pairs:2]
    slack = jnp.minimum(source_of - 1, bound - receiver)
    passed = jax.random.randint(jax.random.fold_in(key, 1), (pairs,), 0, 1 << 20) % (slack + 1)
    sizes = sizes.at[1:1 + 2 * pairs:2].set(source_of - passed).at[2:2 + 2 * pairs:2].set(receiver + passed)
    return sizes[jax.random.permutation(jax.random.fold_in(key, 2), amount)]


def assign_block(key, own, number, rows, amount, top, most, slope):
    sequence = jax.random.permutation(key, amount)
    heavy_load, common = load_shares(amount, rows * top, most, slope, True), load_shares(amount, rows * top, most, slope, False)
    places = jnp.arange(amount)

    def named(lengths, offset_by):
        used = int((lengths > 0).sum())
        fixed = max(1, used // 4)
        moved = fixed + (places - fixed + offset_by * (used - fixed)) % max(1, amount - fixed)
        return jnp.zeros((amount,), jnp.int32).at[sequence[jnp.where(places < fixed, places, moved)]].set(jnp.asarray(lengths, jnp.int32))

    lengths = jnp.where(number % 4 == 0, named(heavy_load, number // 4), named(common, number - number // 4 - 1))
    mixed = jax.random.permutation(jax.random.fold_in(own, 3), amount)
    source_of, receiver = mixed[0:amount // 2 * 2:2], mixed[1:amount // 2 * 2:2]
    margin = jnp.minimum(lengths[source_of] - 1, most - lengths[receiver]) // 2
    margin = jnp.where((source_of == sequence[0]) | (receiver == sequence[0]) | (lengths[receiver] == 0), 0, jnp.maximum(margin, 0))
    moved = jax.random.randint(jax.random.fold_in(own, 4), (amount // 2,), 0, 1 << 20) % (margin + 1)
    lengths = lengths.at[source_of].add(-moved).at[receiver].add(moved)
    labels = jnp.searchsorted(jnp.cumsum(lengths), jnp.arange(rows * top), side="right").astype(jnp.int32)
    table = labels.reshape(top, rows).T
    table = table[jax.random.permutation(jax.random.fold_in(own, 1), rows)]
    offset_by = jax.random.randint(jax.random.fold_in(own, 2), (rows, 1), 0, top)
    return jnp.take_along_axis(table, (jnp.arange(top)[None, :] + offset_by) % top, axis=1)


def load_shares(amount, total, most, lean, full):
    loads = [(1 << 20) // math.isqrt(grade ** lean) + 1 for grade in range(1, amount + 1)]
    largest = most if full else min(most, max(-(-total // amount), total * loads[0] // sum(loads)))
    least = 1 if total - largest >= amount - 1 else 0
    given, surplus = [largest] + [least] * (amount - 1), total - largest - least * (amount - 1)
    while surplus > 0:
        movable = [i for i in range(1, amount) if given[i] < largest] or [i for i in range(1, amount) if given[i] < most]
        mass, budget = sum([loads[i] for i in movable]), surplus
        for i in movable:
            more = min(most - given[i], max(1, budget * loads[i] // mass), surplus)
            given[i] = given[i] + more
            surplus = surplus - more
    return np.array(given)


def scatter_about(key, dims, scale, most, pieces=(), held_as=jnp.bfloat16):
    drawn = jax.random.normal(key, dims, jnp.float32) * scale
    if len(pieces) > 0:
        drawn = steps_of(key, dims, pieces, -0.22, 0.18) * drawn
    return jnp.clip(drawn, min=-most, max=most).astype(held_as)


def setup_inputs(seed: int = 0, part: int = 0) -> dict:
    streams_of = jax.random.split(jax.random.key(seed), 10)
    part_keys = jax.random.split(jax.random.fold_in(streams_of[9], part), 10)
    queries = scatter_about(part_keys[0], (OCTET_TOTAL, HEADS, DK), 1.0, 6.0, ((0, 4), (1, 4)))
    key_rows = scatter_about(part_keys[1], (OCTET_TOTAL, HEADS, DK), 1.0, 6.0, ((0, 4), (1, 4)))
    values = scatter_about(part_keys[2], (OCTET_TOTAL, HEADS, DK), 1.0, 6.0, ((0, 4), (1, 4)))
    log_decay = draw_log_decay(jax.random.fold_in(jax.random.fold_in(streams_of[9], part), 71), part)
    write_rate = jnp.clip(jnp.exp(math.log(0.05) - 3.218876 * jax.random.uniform(part_keys[4], (HEADS, OCTET_TOTAL), jnp.float32) ** steps_of(part_keys[4], (HEADS, OCTET_TOTAL), ((0, 4), (1, 4)), -0.2, 0.2)), 0.002, 0.05)
    router_weight = draw_router_weight(jax.random.fold_in(streams_of[9], 71), part)
    teacher_logits = draw_teacher_logits(jax.random.fold_in(jax.random.fold_in(streams_of[9], part), 71), part)
    span_length = jax.vmap(lambda own: uneven(own, TOK_REG, REGION, MAXLEN, 2))(jax.random.split(part_keys[7], N_SEQ * COLUMNS)).reshape((N_SEQ, COLUMNS, TOK_REG)).astype(jnp.int32)
    span_owner_keys = jax.random.split(jax.random.fold_in(part_keys[8], 1), N_SEQ * COLUMNS * TOK_REG // TOK_REG)
    span_owner_turns = jax.random.permutation(jax.random.fold_in(part_keys[8], 3), N_SEQ * COLUMNS * TOK_REG // TOK_REG)
    span_owner = jax.vmap(lambda own, number: assign_block(jax.random.fold_in(part_keys[8], 2), own, number, TOK_REG, N_SEQ, 1, CAP, 2))(span_owner_keys, span_owner_turns).reshape((N_SEQ, COLUMNS, TOK_REG, 1))
    return dict(queries=queries, key_rows=key_rows, values=values, log_decay=log_decay, write_rate=write_rate, router_weight=router_weight, teacher_logits=teacher_logits, span_length=span_length, span_owner=span_owner)


UPPER_LIMIT = lax.Precision.HIGHEST

def unit_rows(array):
    return array / jnp.sqrt(lax.optimization_barrier(jnp.sum(array * array, axis=-1, keepdims=True)) + 1e-06)

def rounded_units(array):
    lowered = unit_rows(array.astype(jnp.float32)).astype(jnp.bfloat16)
    lowered = lax.optimization_barrier(lowered)
    return lowered.astype(jnp.float32)

def log_probs(logits):
    top = lax.optimization_barrier(jnp.max(logits, axis=-1, keepdims=True))
    displaced_sums = logits - top
    return displaced_sums - jnp.log(lax.optimization_barrier(jnp.sum(jnp.exp(displaced_sums), axis=-1, keepdims=True)))

def reference(queries, key_rows, values, log_decay, write_rate, router_weight, teacher_logits, span_length, span_owner):
    query_unit = rounded_units(queries)
    key_unit = rounded_units(key_rows)
    value_rows = values.astype(jnp.float32)
    decay = jnp.exp(log_decay).T
    rate = write_rate.T

    def advance(recurrent_state, inputs):
        query_current, key_current, value_t, decay_t, rate_t = inputs
        projected_input = jnp.einsum('cq,cqd->cd', key_current, recurrent_state, precision=UPPER_LIMIT)
        erased = recurrent_state - rate_t[:, None, None] * key_current[:, :, None] * projected_input[:, None, :]
        recurrent_state = decay_t[:, None, None] * erased + rate_t[:, None, None] * key_current[:, :, None] * value_t[:, None, :]
        output_rows = jnp.einsum('cq,cqd->cd', query_current, recurrent_state, precision=UPPER_LIMIT)
        return (recurrent_state, output_rows)
    start_state = jnp.zeros((HEADS, DK, DK), jnp.float32)
    _, head_out = lax.scan(advance, start_state, (query_unit, key_unit, value_rows, decay, rate))
    scale = jnp.sqrt(lax.optimization_barrier(jnp.mean(head_out * head_out, axis=-1, keepdims=True)) + 1e-06)
    unit = head_out / scale
    normed = unit.astype(jnp.bfloat16)
    router_f = router_weight.astype(jnp.float32)
    logits = jnp.einsum('lhd,hde->le', normed.astype(jnp.float32), router_f, precision=UPPER_LIMIT)
    region_logits = logits.reshape(N_SEQ, COLUMNS, REGION, E)
    span_start = jnp.cumsum(span_length, axis=-1) - span_length
    positions = jnp.arange(REGION, dtype=jnp.int32)
    member = ((positions >= span_start[..., None]) & (positions < (span_start + span_length)[..., None])).astype(jnp.float32)
    span_len = span_length.astype(jnp.float32)[..., None]
    averaged_groups = jnp.einsum('sctr,scre->scte', member, region_logits, precision=UPPER_LIMIT) / span_len
    owners = span_owner[..., 0]
    token_ids = jnp.arange(TOK_REG, dtype=jnp.int32)
    earlier = token_ids[None, :] < token_ids[:, None]
    same = owners[..., :, None] == owners[..., None, :]
    slot = lax.optimization_barrier(jnp.sum((same & earlier).astype(jnp.int32), axis=-1))
    source = jnp.arange(N_SEQ, dtype=jnp.int32)[:, None, None]
    column = jnp.arange(COLUMNS, dtype=jnp.int32)[None, :, None]
    teacher_tok = teacher_logits[owners, column, source, slot].astype(jnp.float32)
    teacher_lp = log_probs(teacher_tok)
    student_lp = log_probs(averaged_groups)
    teacher_p = jnp.exp(teacher_lp)
    kl_tok = lax.optimization_barrier(jnp.sum(teacher_p * (teacher_lp - student_lp), axis=-1))
    mean_kl = (jnp.sum(kl_tok) / NTOK).reshape(1)
    token_grad = jnp.exp(student_lp) - teacher_p
    row_grad = jnp.einsum('sctr,scte->scre', member, token_grad / span_len, precision=UPPER_LIMIT).astype(jnp.bfloat16)
    row_grad = row_grad.reshape(OCTET_TOTAL, E).astype(jnp.float32)
    grad_router = jnp.einsum('lhd,le->hde', normed.astype(jnp.float32), row_grad, precision=UPPER_LIMIT)
    state_grad = jnp.einsum('le,hde->lhd', row_grad, router_f, precision=UPPER_LIMIT)
    grad_heads = (state_grad - unit * lax.optimization_barrier(jnp.mean(state_grad * unit, axis=-1, keepdims=True))) / scale
    return (grad_router, grad_heads, mean_kl)
```

```python
import functools

import jax
import jax.numpy as jnp
from jax import lax
from jax.experimental import pallas as pl
from jax.experimental.pallas import tpu as pltpu
from jax.sharding import PartitionSpec as P

BLOCK = 128
WIDTH = 128
BASE = 16
PAIR = 2
EXTRA = 16
LIMIT = 48 * 1024 * 1024
UPPER_LIMIT = lax.Precision.HIGHEST
F32 = jnp.float32
BF16 = jnp.bfloat16


def iota(shape, axis):
    return lax.broadcasted_iota(jnp.int32, shape, axis)


def mm(a, b):
    return jnp.dot(a, b, preferred_element_type=F32)


def mm_nt(a, b):
    return lax.dot_general(a, b, (((1,), (1,)), ((), ())), preferred_element_type=F32)


def mm_tn(a, b):
    return lax.dot_general(a, b, (((0,), (0,)), ((), ())), preferred_element_type=F32)


def split(x):
    high = x.astype(BF16)
    return high, (x - high.astype(F32)).astype(BF16)


def dot3(a, b):
    (ah, al), (bh, bl) = a, b
    return mm(jnp.concatenate([ah, al], axis=1), jnp.concatenate([bh, bh], axis=0)) + mm(ah, bl)


def delta_kernel(heads, q_ref, k_ref, v_ref, d_ref, r_ref, loc_ref, reach_ref, x_ref, wide):
    row, col = iota((BLOCK, BLOCK), 0), iota((BLOCK, BLOCK), 1)
    eye, closed, strict = row == col, row >= col, row > col

    @pl.when(pl.program_id(0) == 0)
    def _():
        for h in range(heads):
            x_ref[h] = jnp.concatenate(
                [jnp.zeros((WIDTH, WIDTH), F32), eye.astype(F32)], axis=1
            )

    wide[0] = q_ref[...].astype(F32)
    wide[1] = k_ref[...].astype(F32)
    wide[2] = v_ref[...].astype(F32)
    cells = [(b, h) for b in range(PAIR) for h in range(heads)]

    def unit(x):
        return (x * lax.rsqrt(jnp.sum(x * x, axis=-1, keepdims=True) + 1e-06)).astype(BF16)

    negs, rights, mixers, tails, gq, gends = [], [], [], [], [], []
    for b, h in cells:
        rows = pl.ds(b * BLOCK, BLOCK)
        q = unit(wide[0, rows, h, :])
        k = unit(wide[1, rows, h, :])
        v = wide[2, rows, h, :]
        decay = d_ref[h : h + 1, b * BLOCK : (b + 1) * BLOCK]
        rate = r_ref[h : h + 1, b * BLOCK : (b + 1) * BLOCK]
        cum = jnp.sum(jnp.where(closed, decay, 0.0), axis=1, keepdims=True)
        cum_row = jnp.sum(jnp.where(eye, cum, 0.0), axis=0, keepdims=True)
        rate_col = jnp.sum(jnp.where(eye, rate, 0.0), axis=1, keepdims=True)
        ratio = jnp.exp(jnp.where(closed, cum - cum_row, -1e30))
        gamma = jnp.exp(cum)
        end = cum[BLOCK - 1 : BLOCK, :]
        both = mm_nt(jnp.concatenate([k, q], axis=0), k)
        kf = k.astype(F32)
        negs.append(-(rate_col * jnp.where(strict, ratio * both[:BLOCK], 0.0)))
        rights.append(jnp.concatenate([rate_col * v, (rate_col * gamma) * kf], axis=1))
        mixers.append(ratio * both[BLOCK:])
        tails.append(jnp.transpose(kf * jnp.exp(end - cum)))
        gq.append(gamma * q.astype(F32))
        gends.append(jnp.exp(end))

    n = len(cells)
    same = (row // BASE) == (col // BASE)
    ident = eye.astype(F32)
    diag = [jnp.where(same, x, 0.0) for x in negs]
    inv = [ident + x for x in diag]
    power = [split(x) for x in diag]
    size = 2
    while size < BASE:
        power = [split(dot3(x, x)) for x in power]
        inv = [t + dot3(split(t), p) for t, p in zip(inv, power)]
        size *= 2
    size = BASE
    while size < BLOCK:
        level = ((row // (2 * size)) == (col // (2 * size))) & ((row // size) != (col // size))
        parts = [split(t) for t in inv]
        off = [split(jnp.where(level, x, 0.0)) for x in negs]
        half = [split(dot3(o, p)) for o, p in zip(off, parts)]
        inv = [t + dot3(p, m) for t, p, m in zip(inv, parts, half)]
        size *= 2
    solved = [split(dot3(split(t), split(r))) for t, r in zip(inv, rights)]
    mixed = [
        dot3(split(jnp.concatenate([m, t], axis=0)), s) for m, t, s in zip(mixers, tails, solved)
    ]
    maps = [
        split(
            jnp.concatenate(
                [gq[i] - mixed[i][:BLOCK, WIDTH:], gends[i] * ident - mixed[i][BLOCK:, WIDTH:]],
                axis=0,
            )
        )
        for i in range(n)
    ]
    states = [x_ref[h] for h in range(heads)]
    for i, (b, h) in enumerate(cells):
        rows = pl.ds(b * BLOCK, BLOCK)
        moved = dot3(maps[i], split(states[h]))
        loc_ref[h, rows, :] = moved[:BLOCK, :WIDTH] + mixed[i][:BLOCK, :WIDTH]
        reach_ref[h, rows, :] = moved[:BLOCK, WIDTH:]
        states[h] = jnp.concatenate(
            [moved[BLOCK:, :WIDTH] + mixed[i][BLOCK:, :WIDTH], moved[BLOCK:, WIDTH:]], axis=1
        )
    for h in range(heads):
        x_ref[h] = states[h]


def bounds(lens):
    tok = lens.shape[1]
    row, col = iota((tok, tok), 0), iota((tok, tok), 1)
    start = jnp.sum(jnp.where(col < row, lens, 0.0), axis=1, keepdims=True)
    own = jnp.sum(jnp.where(col == row, lens, 0.0), axis=1, keepdims=True)
    return start, own, row == col


def pool_kernel(heads, lens_ref, loc_ref, reach_ref, s_ref, w_ref, out_ref, sum_ref, log_ref):
    region = loc_ref.shape[1]
    tok = sum_ref.shape[0]
    lens = lens_ref[pl.ds(pl.program_id(0), 1), :].astype(F32)
    start, own, _ = bounds(lens)
    place = iota((tok, region), 1).astype(F32)
    member = ((place >= start) & (place < start + own)).astype(F32).astype(BF16)
    total = jnp.zeros((tok, w_ref.shape[2]), F32)
    for h in range(heads):
        head = loc_ref[h] + dot3(split(reach_ref[h]), split(s_ref[h]))
        out_ref[h] = head
        inverse = lax.rsqrt(jnp.mean(head * head, axis=-1, keepdims=True) + 1e-06)
        summed = mm(member, (head * inverse).astype(BF16))
        sum_ref[:, h * WIDTH : (h + 1) * WIDTH] = summed
        high, low = split(summed)
        total = total + mm(high, w_ref[h]) + mm(low, w_ref[h])
    log_ref[...] = total


def log_probs(x):
    shifted_x = x - jnp.max(x, axis=-1, keepdims=True)
    return shifted_x - jnp.log(jnp.sum(jnp.exp(shifted_x), axis=-1, keepdims=True))


def loss_kernel(cap, lens_ref, own_ref, row_ref, teach_ref, log_ref, g_ref):
    tok = log_ref.shape[0]
    experts = log_ref.shape[1]
    _, own, _ = bounds(lens_ref[...].astype(F32))
    row, col = iota((tok, tok), 0), iota((tok, tok), 1)
    earlier = ((own_ref[...] == row_ref[...]) & (col < row)).astype(F32)
    slot = jnp.sum(earlier, axis=1, keepdims=True)
    target = own_ref[...].astype(F32) * cap + slot
    count = teach_ref.shape[0]
    pick = (iota((tok, count), 1).astype(F32) == target).astype(F32).astype(BF16)
    teacher_lp = log_probs(mm(pick, teach_ref[...]))
    student_lp = log_probs(log_ref[...] / own)
    prob = jnp.exp(teacher_lp)
    kl = jnp.sum(prob * (teacher_lp - student_lp), axis=-1, keepdims=True)
    kl = jnp.sum(kl, axis=0, keepdims=True)
    g_ref[0:tok, :] = ((jnp.exp(student_lp) - prob) / own).astype(BF16)
    high, rest = split(kl)
    low = kl - high.astype(F32) - rest.astype(F32)
    line = iota((EXTRA, experts), 0)
    g_ref[tok : tok + EXTRA, :] = jnp.where(
        line == 0, high.astype(F32), jnp.where(line == 1, rest.astype(F32), jnp.where(line == 2, low, 0.0))
    ).astype(BF16)


def router_kernel(regions, sum_ref, g_ref, out_ref):
    tok = sum_ref.shape[0] // regions
    wide = sum_ref.shape[1]
    total = jnp.zeros((wide, g_ref.shape[1]), F32)
    kl = jnp.zeros((EXTRA, g_ref.shape[1]), F32)
    for r in range(regions):
        first = r * (tok + EXTRA)
        g = g_ref[first : first + tok, :]
        high, low = split(sum_ref[r * tok : (r + 1) * tok, :])
        total = total + mm_tn(jnp.concatenate([high, low], axis=0), jnp.concatenate([g, g], axis=0))
        kl = kl + g_ref[first + tok : first + tok + EXTRA, :].astype(F32)
    out_ref[0:wide, :] = total
    out_ref[wide : wide + 8, :] = jnp.broadcast_to(
        jnp.sum(kl, axis=0, keepdims=True), (8, g_ref.shape[1])
    )


def heads_kernel(heads, lens_ref, head_ref, g_ref, w_ref, out_ref):
    region = head_ref.shape[1]
    tok = lens_ref.shape[1]
    lens = lens_ref[pl.ds(pl.program_id(0), 1), :].astype(F32)
    start, _, eye = bounds(lens)
    start_row = jnp.sum(jnp.where(eye, start, 0.0), axis=0, keepdims=True)
    place = iota((region, tok), 0).astype(F32)
    member = ((place >= start_row) & (place < start_row + lens)).astype(F32).astype(BF16)
    g = g_ref[0:tok, :]
    for h in range(heads):
        high, low = split(mm_nt(g, w_ref[h]))
        grad = mm(member, high) + mm(member, low)
        head = head_ref[h]
        inverse = lax.rsqrt(jnp.mean(head * head, axis=-1, keepdims=True) + 1e-06)
        unit = head * inverse
        mean = jnp.mean(grad * unit, axis=-1, keepdims=True)
        out_ref[:, h, :] = (grad - unit * mean) * inverse


def shifted(value, axis, steps):
    count = lax.axis_size(axis)
    return lax.ppermute(value, axis, [(source, source + steps) for source in range(count - steps)])


def params():
    return pltpu.CompilerParams(vmem_limit_bytes=LIMIT)


def cost(flops, size):
    return pl.CostEstimate(flops=flops, bytes_accessed=size, transcendentals=0)


def shards(
    queries,
    key_rows,
    values,
    log_decay,
    write_rate,
    router_weight,
    teacher_logits,
    span_length,
    span_owner,
):
    rows, heads, width = queries.shape
    regions = lax.axis_size(("head", "tp"))
    region = rows // regions
    lens = span_length.reshape(1, -1)
    tok = lens.shape[1]
    n_seq = lax.axis_size("seq")
    cap = teacher_logits.shape[3]
    experts = teacher_logits.shape[4]
    sds = jax.ShapeDtypeStruct

    teacher = lax.all_to_all(
        teacher_logits.reshape(n_seq, cap, experts), "seq", split_axis=0, concat_axis=0, tiled=True
    ).reshape(n_seq * cap, experts)
    lens_all = lax.all_gather(lens, ("head", "tp"), axis=0, tiled=True)

    step = PAIR * BLOCK
    whole = lambda shape: pl.BlockSpec(shape, lambda i: (0,) * len(shape))
    by_rows = pl.BlockSpec((step, heads, width), lambda i: (i, 0, 0))
    by_lane = pl.BlockSpec((heads, step), lambda i: (0, i))
    by_head = pl.BlockSpec((heads, step, width), lambda i: (0, i, 0))
    local, reach, ends = pl.pallas_call(
        functools.partial(delta_kernel, heads),
        grid=(rows // step,),
        in_specs=[by_rows, by_rows, by_rows, by_lane, by_lane],
        out_specs=[by_head, by_head, whole((heads, width, 2 * width))],
        out_shape=[
            sds((heads, rows, width), F32),
            sds((heads, rows, width), F32),
            sds((heads, width, 2 * width), F32),
        ],
        scratch_shapes=[pltpu.VMEM((3, step, heads, width), F32)],
        compiler_params=params(),
        cost_estimate=cost(30_000_000_000, 20_000_000),
        name="delta",
    )(queries, key_rows, values, log_decay, write_rate)
    dev_add, dev_map = ends[:, :, :width], ends[:, :, width:]

    state = shifted(dev_add, "seq", 1) if n_seq > 1 else jnp.zeros_like(dev_add)
    for _ in range(n_seq - 2):
        moved = jnp.einsum("hij,hjk->hik", dev_map, state, precision=UPPER_LIMIT) + dev_add
        state = shifted(moved, "seq", 1)

    by_region = pl.BlockSpec((heads, region, width), lambda i: (0, i, 0))
    head_out, sums, partial = pl.pallas_call(
        functools.partial(pool_kernel, heads),
        grid=(regions,),
        in_specs=[
            whole((regions, tok)),
            by_region,
            by_region,
            whole((heads, width, width)),
            whole((heads, width, experts)),
        ],
        out_specs=[
            by_region,
            pl.BlockSpec((tok, heads * width), lambda i: (i, 0)),
            pl.BlockSpec((tok, experts), lambda i: (i, 0)),
        ],
        out_shape=[
            sds((heads, rows, width), F32),
            sds((regions * tok, heads * width), F32),
            sds((regions * tok, experts), F32),
        ],
        compiler_params=params(),
        cost_estimate=cost(3_000_000_000, 16_000_000),
        name="pool",
    )(lens_all, local, reach, state, router_weight)

    summed = lax.psum_scatter(partial, ("head", "tp"), scatter_dimension=0, tiled=True)
    grads = pl.pallas_call(
        functools.partial(loss_kernel, cap),
        out_shape=sds((tok + EXTRA, experts), BF16),
        compiler_params=params(),
        name="loss",
    )(lens, span_owner.reshape(tok, 1), span_owner.reshape(1, tok), teacher, summed)
    gathered = lax.all_gather(grads, ("head", "tp"), axis=0, tiled=True)

    router = pl.pallas_call(
        functools.partial(router_kernel, regions),
        out_shape=sds((heads * width + 8, experts), F32),
        compiler_params=params(),
        cost_estimate=cost(300_000_000, 2_000_000),
        name="router",
    )(sums, gathered)
    router = lax.psum(router, "seq")
    grad_heads = pl.pallas_call(
        functools.partial(heads_kernel, heads),
        grid=(regions,),
        in_specs=[
            whole((regions, tok)),
            by_region,
            pl.BlockSpec((tok + EXTRA, experts), lambda i: (i, 0)),
            whole((heads, width, experts)),
        ],
        out_specs=pl.BlockSpec((region, heads, width), lambda i: (i, 0, 0)),
        out_shape=sds((rows, heads, width), F32),
        compiler_params=params(),
        cost_estimate=cost(3_000_000_000, 12_000_000),
        name="heads",
    )(lens_all, head_out, gathered, router_weight)
    grad_router = router[: heads * width].reshape(heads, width, experts)
    mean_kl = router[heads * width, :1] / (tok * n_seq * regions)
    return (grad_router, grad_heads, mean_kl)


def solution(mesh):
    placed = (
        P(("grp", "seq"), ("head", "tp"), None),
        P(("grp", "seq"), ("head", "tp"), None),
        P(("grp", "seq"), ("head", "tp"), None),
        P(("head", "tp"), ("grp", "seq")),
        P(("head", "tp"), ("grp", "seq")),
        P(("head", "tp"), None, None),
        P(("grp", "seq"), ("head", "tp"), None, None, None),
        P(("grp", "seq"), ("head", "tp"), None),
        P(("grp", "seq"), ("head", "tp"), None, None),
    )
    return jax.shard_map(
        shards,
        mesh=mesh,
        in_specs=placed,
        out_specs=(
            P(("grp", "head", "tp"), None, None),
            P(("grp", "seq"), ("head", "tp"), None),
            P("grp"),
        ),
        check_vma=False,
    )
```

```python
import functools

import jax
import jax.numpy as jnp
from jax import lax
from jax.experimental import pallas as pl
from jax.experimental.pallas import tpu as pltpu
from jax.sharding import PartitionSpec as P

BLOCK = 128
WIDTH = 128
BASE = 16
PAIR = 2
EXTRA = 16
LIMIT = 48 * 1024 * 1024
UPPER_LIMIT = lax.Precision.HIGHEST
F32 = jnp.float32
BF16 = jnp.bfloat16


def iota(shape, axis):
    return lax.broadcasted_iota(jnp.int32, shape, axis)


def mm(a, b):
    return jnp.dot(a, b, preferred_element_type=F32)


def mm_nt(a, b):
    return lax.dot_general(a, b, (((1,), (1,)), ((), ())), preferred_element_type=F32)


def mm_tn(a, b):
    return lax.dot_general(a, b, (((0,), (0,)), ((), ())), preferred_element_type=F32)


def split(x):
    high = x.astype(BF16)
    return high, (x - high.astype(F32)).astype(BF16)


def dot3(a, b):
    (ah, al), (bh, bl) = a, b
    return mm(jnp.concatenate([ah, al], axis=1), jnp.concatenate([bh, bh], axis=0)) + mm(ah, bl)


def delta_kernel(heads, q_ref, k_ref, v_ref, d_ref, r_ref, loc_ref, reach_ref, x_ref, wide):
    row, col = iota((BLOCK, BLOCK), 0), iota((BLOCK, BLOCK), 1)
    eye, closed, strict = row == col, row >= col, row > col

    @pl.when(pl.program_id(0) == 0)
    def _():
        for h in range(heads):
            x_ref[h] = jnp.concatenate(
                [jnp.zeros((WIDTH, WIDTH), F32), eye.astype(F32)], axis=1
            )

    wide[0] = q_ref[...].astype(F32)
    wide[1] = k_ref[...].astype(F32)
    wide[2] = v_ref[...].astype(F32)
    cells = [(b, h) for b in range(PAIR) for h in range(heads)]

    def unit(x):
        return (x * lax.rsqrt(jnp.sum(x * x, axis=-1, keepdims=True) + 1e-06)).astype(BF16)

    negs, rights, mixers, tails, gq, gends = [], [], [], [], [], []
    for b, h in cells:
        rows = pl.ds(b * BLOCK, BLOCK)
        q = unit(wide[0, rows, h, :])
        k = unit(wide[1, rows, h, :])
        v = wide[2, rows, h, :]
        decay = d_ref[h : h + 1, b * BLOCK : (b + 1) * BLOCK]
        rate = r_ref[h : h + 1, b * BLOCK : (b + 1) * BLOCK]
        cum = jnp.sum(jnp.where(closed, decay, 0.0), axis=1, keepdims=True)
        cum_row = jnp.sum(jnp.where(eye, cum, 0.0), axis=0, keepdims=True)
        rate_col = jnp.sum(jnp.where(eye, rate, 0.0), axis=1, keepdims=True)
        ratio = jnp.exp(jnp.where(closed, cum - cum_row, -1e30))
        gamma = jnp.exp(cum)
        end = cum[BLOCK - 1 : BLOCK, :]
        both = mm_nt(jnp.concatenate([k, q], axis=0), k)
        kf = k.astype(F32)
        negs.append(-(rate_col * jnp.where(strict, ratio * both[:BLOCK], 0.0)))
        rights.append(jnp.concatenate([rate_col * v, (rate_col * gamma) * kf], axis=1))
        mixers.append(ratio * both[BLOCK:])
        tails.append(jnp.transpose(kf * jnp.exp(end - cum)))
        gq.append(gamma * q.astype(F32))
        gends.append(jnp.exp(end))

    n = len(cells)
    same = (row // BASE) == (col // BASE)
    ident = eye.astype(F32)
    diag = [jnp.where(same, x, 0.0) for x in negs]
    inv = [ident + x for x in diag]
    power = [split(x) for x in diag]
    size = 2
    while size < BASE:
        power = [split(dot3(x, x)) for x in power]
        inv = [t + dot3(split(t), p) for t, p in zip(inv, power)]
        size *= 2
    size = BASE
    while size < BLOCK:
        level = ((row // (2 * size)) == (col // (2 * size))) & ((row // size) != (col // size))
        parts = [split(t) for t in inv]
        off = [split(jnp.where(level, x, 0.0)) for x in negs]
        half = [split(dot3(o, p)) for o, p in zip(off, parts)]
        inv = [t + dot3(p, m) for t, p, m in zip(inv, parts, half)]
        size *= 2
    solved = [split(dot3(split(t), split(r))) for t, r in zip(inv, rights)]
    mixed = [
        dot3(split(jnp.concatenate([m, t], axis=0)), s) for m, t, s in zip(mixers, tails, solved)
    ]
    maps = [
        split(
            jnp.concatenate(
                [gq[i] - mixed[i][:BLOCK, WIDTH:], gends[i] * ident - mixed[i][BLOCK:, WIDTH:]],
                axis=0,
            )
        )
        for i in range(n)
    ]
    states = [x_ref[h] for h in range(heads)]
    for i, (b, h) in enumerate(cells):
        rows = pl.ds(b * BLOCK, BLOCK)
        moved = dot3(maps[i], split(states[h]))
        loc_ref[h, rows, :] = moved[:BLOCK, :WIDTH] + mixed[i][:BLOCK, :WIDTH]
        reach_ref[h, rows, :] = moved[:BLOCK, WIDTH:]
        states[h] = jnp.concatenate(
            [moved[BLOCK:, :WIDTH] + mixed[i][BLOCK:, :WIDTH], moved[BLOCK:, WIDTH:]], axis=1
        )
    for h in range(heads):
        x_ref[h] = states[h]


def bounds(lens):
    tok = lens.shape[1]
    row, col = iota((tok, tok), 0), iota((tok, tok), 1)
    start = jnp.sum(jnp.where(col < row, lens, 0.0), axis=1, keepdims=True)
    own = jnp.sum(jnp.where(col == row, lens, 0.0), axis=1, keepdims=True)
    return start, own, row == col


def pool_kernel(heads, lens_ref, loc_ref, reach_ref, s_ref, w_ref, out_ref, sum_ref, log_ref):
    region = loc_ref.shape[1]
    tok = sum_ref.shape[0]
    lens = lens_ref[pl.ds(pl.program_id(0), 1), :].astype(F32)
    start, own, _ = bounds(lens)
    place = iota((tok, region), 1).astype(F32)
    member = ((place >= start) & (place < start + own)).astype(F32).astype(BF16)
    total = jnp.zeros((tok, w_ref.shape[2]), F32)
    for h in range(heads):
        head = loc_ref[h] + dot3(split(reach_ref[h]), split(s_ref[h]))
        out_ref[h] = head
        inverse = lax.rsqrt(jnp.mean(head * head, axis=-1, keepdims=True) + 1e-06)
        summed = mm(member, (head * inverse).astype(BF16))
        sum_ref[:, h * WIDTH : (h + 1) * WIDTH] = summed
        high, low = split(summed)
        total = total + mm(high, w_ref[h]) + mm(low, w_ref[h])
    log_ref[...] = total


def log_probs(x):
    shifted_x = x - jnp.max(x, axis=-1, keepdims=True)
    return shifted_x - jnp.log(jnp.sum(jnp.exp(shifted_x), axis=-1, keepdims=True))


MESH = pl.DeviceIdType.MESH


def tile_place(index):
    count = lax.axis_size("tp")
    return {"head": index // count, "tp": lax.rem(index, count)}


def signal(barrier, device):
    pl.semaphore_signal(barrier, inc=1, device_id=device, device_id_type=MESH)


def send(source, target, sems, slot, device):
    return pltpu.make_async_remote_copy(
        src_ref=source,
        dst_ref=target,
        send_sem=sems.at[0, slot],
        recv_sem=sems.at[1, slot],
        device_id=device,
        device_id_type=MESH,
    )


def relay_kernel(heads, n_seq, regions, ends_ref, lens_ref, s_ref, all_ref, came, gone, lbuf, sems, lsems):
    me = lax.axis_index("seq")
    tile = lax.axis_index("head") * lax.axis_size("tp") + lax.axis_index("tp")
    barrier = pltpu.get_barrier_semaphore()

    for o in (1, n_seq - 1):
        signal(barrier, {"seq": lax.rem(me + o, n_seq)})
    for o in range(1, regions):
        signal(barrier, tile_place(lax.rem(tile + o, regions)))
    pl.semaphore_wait(barrier, regions + 1)

    def hop(h):
        return send(gone.at[h], came.at[h], sems, h, {"seq": lax.rem(me + 1, n_seq)})

    @pl.when(me == 0)
    def _():
        for h in range(heads):
            gone[h] = ends_ref[h, :, :WIDTH]
            hop(h).start()
        s_ref[...] = jnp.zeros_like(s_ref)

    lens_copies = [
        send(lens_ref, lbuf.at[tile], lsems, o, tile_place(lax.rem(tile + o, regions)))
        for o in range(1, regions)
    ]
    for copy in lens_copies:
        copy.start()
    lbuf[tile] = lens_ref[...]

    @pl.when(me > 0)
    def _():
        for h in range(heads):
            hop(h).wait_recv()
            state = came[h]
            s_ref[h] = state

            @pl.when(me < n_seq - 1)
            def _():
                gone[h] = dot3(split(ends_ref[h, :, WIDTH:]), split(state)) + ends_ref[h, :, :WIDTH]
                hop(h).start()

    for copy in lens_copies:
        copy.wait()
    for r in range(regions):
        all_ref[r : r + 1, :] = lbuf[r, 0:1, :]

    @pl.when(me < n_seq - 1)
    def _():
        for h in range(heads):
            hop(h).wait_send()


def loss_kernel(
    cap, n_seq, regions, lens_ref, own_ref, row_ref, teach_ref, log_ref, out_ref, tbuf, lbuf, gbuf, tsems, lsems, gsems
):
    experts = log_ref.shape[1]
    tok = log_ref.shape[0] // regions
    me = lax.axis_index("seq")
    tile = lax.axis_index("head") * lax.axis_size("tp") + lax.axis_index("tp")
    barrier = pltpu.get_barrier_semaphore()
    for o in range(1, regions):
        signal(barrier, tile_place(lax.rem(tile + o, regions)))
    for o in range(1, n_seq):
        signal(barrier, {"seq": lax.rem(me + o, n_seq)})
    pl.semaphore_wait(barrier, regions + n_seq - 2)
    logs, teachers = [], []
    for o in range(1, regions):
        peer = lax.rem(tile + o, regions)
        part = log_ref.at[pl.ds(pl.multiple_of(peer * tok, tok), tok), :]
        logs.append(send(part, lbuf.at[o], lsems, o, tile_place(peer)))
        logs[-1].start()
    for o in range(1, n_seq):
        peer = lax.rem(me + o, n_seq)
        teachers.append(send(teach_ref.at[peer], tbuf.at[me], tsems, o, {"seq": peer}))
        teachers[-1].start()
    tbuf[me] = teach_ref[me]

    _, own, _ = bounds(lens_ref[...].astype(F32))
    row, col = iota((tok, tok), 0), iota((tok, tok), 1)
    earlier = ((own_ref[...] == row_ref[...]) & (col < row)).astype(F32)
    slot = jnp.sum(earlier, axis=1, keepdims=True)
    owner = own_ref[...].astype(F32)
    for copy in teachers:
        copy.wait()
    width = tbuf.shape[1]
    teacher = jnp.zeros((tok, experts), F32)
    for j in range(n_seq):
        pick = (owner == j) & (iota((tok, width), 1).astype(F32) == slot)
        teacher = teacher + mm(pick.astype(F32).astype(BF16), tbuf[j])
    teacher_lp = log_probs(teacher)
    prob = jnp.exp(teacher_lp)

    total = log_ref[pl.ds(pl.multiple_of(tile * tok, tok), tok), :]
    for o, copy in enumerate(logs):
        copy.wait()
        total = total + lbuf[o + 1]
    student_lp = log_probs(total / own)
    kl = jnp.sum(prob * (teacher_lp - student_lp), axis=-1, keepdims=True)
    kl = jnp.sum(kl, axis=0, keepdims=True)
    grad = ((jnp.exp(student_lp) - prob) / own).astype(BF16)
    high, rest = split(kl)
    low = kl - high.astype(F32) - rest.astype(F32)
    line = iota((EXTRA, experts), 0)
    tail = jnp.where(
        line == 0, high.astype(F32), jnp.where(line == 1, rest.astype(F32), jnp.where(line == 2, low, 0.0))
    ).astype(BF16)
    gbuf[tile] = jnp.concatenate([grad, tail], axis=0)
    copies = [
        send(gbuf.at[tile], gbuf.at[tile], gsems, o, tile_place(lax.rem(tile + o, regions)))
        for o in range(1, regions)
    ]
    for copy in copies:
        copy.start()
    for copy in copies:
        copy.wait()
    for r in range(regions):
        out_ref[r * (tok + EXTRA) : (r + 1) * (tok + EXTRA), :] = gbuf[r]


def router_kernel(regions, n_seq, sum_ref, g_ref, out_ref, kl_ref, mine, came, done, asems, bsems):
    tok = sum_ref.shape[0] // regions
    wide = sum_ref.shape[1]
    part = wide // n_seq
    me = lax.axis_index("seq")
    barrier = pltpu.get_barrier_semaphore()
    for o in range(1, n_seq):
        signal(barrier, {"seq": lax.rem(me + o, n_seq)})
    total = jnp.zeros((wide, g_ref.shape[1]), F32)
    kl = jnp.zeros((EXTRA, g_ref.shape[1]), F32)
    for r in range(regions):
        first = r * (tok + EXTRA)
        g = g_ref[first : first + tok, :]
        high, low = split(sum_ref[r * tok : (r + 1) * tok, :])
        total = total + mm_tn(jnp.concatenate([high, low], axis=0), jnp.concatenate([g, g], axis=0))
        kl = kl + g_ref[first + tok : first + tok + EXTRA, :].astype(F32)
    kl = jnp.broadcast_to(jnp.sum(kl, axis=0, keepdims=True), (8, g_ref.shape[1]))
    for p in range(n_seq):
        mine[p, 0:part, :] = total[p * part : (p + 1) * part]
        mine[p, part : part + 8, :] = kl
    pl.semaphore_wait(barrier, n_seq - 1)
    copies = []
    for o in range(1, n_seq):
        peer = lax.rem(me + o, n_seq)
        copies.append(send(mine.at[peer], came.at[o], asems, o, {"seq": peer}))
        copies[-1].start()
    summed = mine[me]
    for o, copy in enumerate(copies):
        copy.wait()
        summed = summed + came[o + 1]
    done[me] = summed
    copies = []
    for o in range(1, n_seq):
        copies.append(send(done.at[me], done.at[me], bsems, o, {"seq": lax.rem(me + o, n_seq)}))
        copies[-1].start()
    for copy in copies:
        copy.wait()
    for p in range(n_seq):
        out_ref[p * part : (p + 1) * part, :] = done[p, 0:part, :]
    kl_ref[...] = done[0, part : part + 8, 0:128]


def heads_kernel(heads, lens_ref, head_ref, g_ref, w_ref, out_ref):
    region = head_ref.shape[1]
    tok = lens_ref.shape[1]
    lens = lens_ref[pl.ds(pl.program_id(0), 1), :].astype(F32)
    start, _, eye = bounds(lens)
    start_row = jnp.sum(jnp.where(eye, start, 0.0), axis=0, keepdims=True)
    place = iota((region, tok), 0).astype(F32)
    member = ((place >= start_row) & (place < start_row + lens)).astype(F32).astype(BF16)
    g = g_ref[0:tok, :]
    for h in range(heads):
        high, low = split(mm_nt(g, w_ref[h]))
        grad = mm(member, high) + mm(member, low)
        head = head_ref[h]
        inverse = lax.rsqrt(jnp.mean(head * head, axis=-1, keepdims=True) + 1e-06)
        unit = head * inverse
        mean = jnp.mean(grad * unit, axis=-1, keepdims=True)
        out_ref[:, h, :] = (grad - unit * mean) * inverse


def params(number=None):
    if number is None:
        return pltpu.CompilerParams(vmem_limit_bytes=LIMIT)
    return pltpu.CompilerParams(
        vmem_limit_bytes=LIMIT, collective_id=number, has_side_effects=True
    )


def cost(flops, size):
    return pl.CostEstimate(flops=flops, bytes_accessed=size, transcendentals=0)


def shards(
    queries,
    key_rows,
    values,
    log_decay,
    write_rate,
    router_weight,
    teacher_logits,
    span_length,
    span_owner,
):
    rows, heads, width = queries.shape
    regions = lax.axis_size(("head", "tp"))
    region = rows // regions
    lens = span_length.reshape(1, -1)
    tok = lens.shape[1]
    n_seq = lax.axis_size("seq")
    cap = teacher_logits.shape[3]
    experts = teacher_logits.shape[4]
    sds = jax.ShapeDtypeStruct
    slots = -(-cap // 16) * 16
    teacher = teacher_logits.reshape(n_seq, cap, experts)
    if slots > cap:
        teacher = jnp.pad(teacher, ((0, 0), (0, slots - cap), (0, 0)))

    tile_sems = pltpu.SemaphoreType.DMA((2, regions))
    seq_sems = pltpu.SemaphoreType.DMA((2, n_seq))
    step = PAIR * BLOCK
    whole = lambda shape: pl.BlockSpec(shape, lambda i: (0,) * len(shape))
    by_rows = pl.BlockSpec((step, heads, width), lambda i: (i, 0, 0))
    by_lane = pl.BlockSpec((heads, step), lambda i: (0, i))
    by_head = pl.BlockSpec((heads, step, width), lambda i: (0, i, 0))
    local, reach, ends = pl.pallas_call(
        functools.partial(delta_kernel, heads),
        grid=(rows // step,),
        in_specs=[by_rows, by_rows, by_rows, by_lane, by_lane],
        out_specs=[by_head, by_head, whole((heads, width, 2 * width))],
        out_shape=[
            sds((heads, rows, width), F32),
            sds((heads, rows, width), F32),
            sds((heads, width, 2 * width), F32),
        ],
        scratch_shapes=[pltpu.VMEM((3, step, heads, width), F32)],
        compiler_params=params(),
        cost_estimate=cost(30_000_000_000, 20_000_000),
        name="delta",
    )(queries, key_rows, values, log_decay, write_rate)
    lanes = -(-tok // 128) * 128
    state, lens_all = pl.pallas_call(
        functools.partial(relay_kernel, heads, n_seq, regions),
        out_shape=[sds((heads, width, width), F32), sds((regions, lanes), jnp.int32)],
        scratch_shapes=[
            pltpu.VMEM((heads, width, width), F32),
            pltpu.VMEM((heads, width, width), F32),
            pltpu.VMEM((regions, 8, lanes), jnp.int32),
            pltpu.SemaphoreType.DMA((2, heads)),
            tile_sems,
        ],
        compiler_params=params(1),
        name="relay",
    )(ends, jnp.broadcast_to(jnp.pad(lens, ((0, 0), (0, lanes - tok))), (8, lanes)))
    lens_all = lens_all[:, :tok]

    by_region = pl.BlockSpec((heads, region, width), lambda i: (0, i, 0))
    head_out, sums, partial = pl.pallas_call(
        functools.partial(pool_kernel, heads),
        grid=(regions,),
        in_specs=[
            whole((regions, tok)),
            by_region,
            by_region,
            whole((heads, width, width)),
            whole((heads, width, experts)),
        ],
        out_specs=[
            by_region,
            pl.BlockSpec((tok, heads * width), lambda i: (i, 0)),
            pl.BlockSpec((tok, experts), lambda i: (i, 0)),
        ],
        out_shape=[
            sds((heads, rows, width), F32),
            sds((regions * tok, heads * width), F32),
            sds((regions * tok, experts), F32),
        ],
        compiler_params=params(),
        cost_estimate=cost(3_000_000_000, 16_000_000),
        name="pool",
    )(lens_all, local, reach, state, router_weight)

    gathered = pl.pallas_call(
        functools.partial(loss_kernel, cap, n_seq, regions),
        out_shape=sds((regions * (tok + EXTRA), experts), BF16),
        scratch_shapes=[
            pltpu.VMEM((n_seq, slots, experts), BF16),
            pltpu.VMEM((regions, tok, experts), F32),
            pltpu.VMEM((regions, tok + EXTRA, experts), BF16),
            seq_sems,
            tile_sems,
            tile_sems,
        ],
        compiler_params=params(2),
        name="loss",
    )(lens, span_owner.reshape(tok, 1), span_owner.reshape(1, tok), teacher, partial)

    router, kl = pl.pallas_call(
        functools.partial(router_kernel, regions, n_seq),
        out_shape=[sds((heads * width, experts), F32), sds((8, 128), F32)],
        scratch_shapes=[pltpu.VMEM((n_seq, heads * width // n_seq + 8, experts), F32)] * 3
        + [seq_sems, seq_sems],
        compiler_params=params(3),
        cost_estimate=cost(300_000_000, 2_000_000),
        name="router",
    )(sums, gathered)
    grad_heads = pl.pallas_call(
        functools.partial(heads_kernel, heads),
        grid=(regions,),
        in_specs=[
            whole((regions, tok)),
            by_region,
            pl.BlockSpec((tok + EXTRA, experts), lambda i: (i, 0)),
            whole((heads, width, experts)),
        ],
        out_specs=pl.BlockSpec((region, heads, width), lambda i: (i, 0, 0)),
        out_shape=sds((rows, heads, width), F32),
        compiler_params=params(),
        cost_estimate=cost(3_000_000_000, 12_000_000),
        name="heads",
    )(lens_all, head_out, gathered, router_weight)
    grad_router = router.reshape(heads, width, experts)
    mean_kl = kl[0, :1] / (tok * n_seq * regions)
    return (grad_router, grad_heads, mean_kl)


def solution(mesh):
    placed = (
        P(("grp", "seq"), ("head", "tp"), None),
        P(("grp", "seq"), ("head", "tp"), None),
        P(("grp", "seq"), ("head", "tp"), None),
        P(("head", "tp"), ("grp", "seq")),
        P(("head", "tp"), ("grp", "seq")),
        P(("head", "tp"), None, None),
        P(("grp", "seq"), ("head", "tp"), None, None, None),
        P(("grp", "seq"), ("head", "tp"), None),
        P(("grp", "seq"), ("head", "tp"), None, None),
    )
    return jax.shard_map(
        shards,
        mesh=mesh,
        in_specs=placed,
        out_specs=(
            P(("grp", "head", "tp"), None, None),
            P(("grp", "seq"), ("head", "tp"), None),
            P("grp"),
        ),
        check_vma=False,
    )
```
